128 devices in a mesh: src: 16 (over z_hi, x, core), snode: 8 (over y, z_lo).
Axes of the slice: x: 4, y: 4, z: 4 (z_hi: 2, z_lo: 2; z = z_hi * 2 + z_lo), core: 2. Of those that a mesh axis runs over, the one named last changes fastest.
Arguments:
- leaf_rhs: float32 [64, 256, 2048], P('snode', None, 'src'), may hold values from -6 to 6
- top_rhs: float32 [2048, 2048], P(None, 'src'), may hold values from -6 to 6
- leaf_inv: float32 [64, 256, 256], P('snode'), may hold values from -1 to 1, as said below
- coupling: float32 [64, 2048, 256], P('snode'), may hold values from -0.046875 to 0.046875
- top_inv: float32 [2048, 2048], P('snode'), may hold values from -1 to 1, as said below
- cond: float32 [64, 256], P('snode'), may hold values from 0.1 to 3
- electrodes: int32 [8192, 4], P('src'), may hold values from 0 to 2047, all different within a row
- blocks: int32 [16, 8192], P(None, 'src'), may hold values from 0 to 63
Outputs:
- sens: float32 [16, 256, 8192], P('snode', None, 'src')
The draws below stay inside these ranges and needn't reach their ends.
Inputs may be any that keep to these rules, and one draw needn't show every extreme that they name: `electrodes`: the four sources of a row are different. `leaf_inv`: zero above the diagonal of each block. `top_inv`: zero above the diagonal.
All inputs are finite; a program needn't handle non-finite values.
Results may differ from the reference program's by a relative error of at most 0.00011.
Values sent between devices are 32-bit elements; how exact they have to be, the bound alone decides.
No kernel may reach another device: no remote copies, remote signals or barrier semaphores. Data moves between devices by JAX's collectives and lax.ppermute only.
A program may use at most 320 MiB of HBM per device.

```python
import math
import jax
import jax.numpy as jnp
import numpy as np
from jax import lax

W = 256
NBLK = 64
S = 2048
NS = 2048
NQ = 8192
KB = 16


def triangle(key, number, extent):
    diag_key, off_key = jax.random.split(key)
    diagonal = jax.random.uniform(diag_key, (number, extent), jnp.float32, 0.5, 1.0)
    spread = jax.random.normal(off_key, (number, extent, extent), jnp.float32)
    spread = jnp.clip(spread * (0.6 / math.sqrt(extent)), -1.0, 1.0)
    row_ids = lax.broadcasted_iota(jnp.int32, (extent, extent), 0)
    col_ids = lax.broadcasted_iota(jnp.int32, (extent, extent), 1)
    strict = (row_ids > col_ids).astype(jnp.float32)
    unit_diag = (row_ids == col_ids).astype(jnp.float32)
    return spread * strict[None] + diagonal[:, :, None] * unit_diag[None]


def draw_leaf_inv(key, part):
    return triangle(key, NBLK, W)


def draw_top_inv(key, part):
    return triangle(key, 1, S)[0]


def set_ends(array, own_key, least, high):
    place = [jax.random.randint(jax.random.fold_in(own_key, axis), (), 0, length) for axis, length in enumerate(array.shape)]
    longest = array.shape.index(max(array.shape))
    neighbour = place[:longest] + [(place[longest] + 1) % array.shape[longest]] + place[longest + 1:]
    return array.at[tuple(place)].set(least).at[tuple(neighbour)].set(high)


def block_scale(own_key, shape, pieces, smallest, high):
    def one(axis_at, shards_of):
        heights = jax.random.uniform(jax.random.fold_in(jax.random.fold_in(own_key, 6), axis_at), (shards_of,), jnp.float32, smallest / len(pieces), high / len(pieces))
        return jnp.repeat(jnp.exp(heights), shape[axis_at] // shards_of).reshape((-1,) + (1,) * (len(shape) - axis_at - 1))

    loudness = one(*pieces[0])
    for cut in pieces[1:]:
        loudness = loudness * one(*cut)
    return loudness


def rank_table(number_of, skew):
    portions = [(1 << 20) // math.isqrt(standing ** skew) + 1 for standing in range(1, number_of + 1)]
    scale = 1 + sum(portions) // (1 << 30)
    return np.cumsum(np.array([max(1, weight // scale) for weight in portions]))


def ranked_ids(rng, dims, number_of, slope):
    listing = rank_table(number_of, slope)
    lot = jax.random.randint(jax.random.fold_in(rng, 1), dims, 0, int(listing[number_of - 1]))
    rank = jnp.searchsorted(jnp.asarray(listing, jnp.int32), lot, side="right")
    return jax.random.permutation(jax.random.fold_in(rng, 2), number_of)[rank].astype(jnp.int32)


def picks_of(key, rows, count, top, lift):
    sequence = jax.random.permutation(jax.random.fold_in(key, 1), count)
    boost = sequence
    for power in range(3):
        boost = boost * boost // count
    boost = boost * lift // count
    chance = jax.random.randint(jax.random.fold_in(key, 2), (rows, count), 0, 4096) + boost
    fixed_rows = jax.random.permutation(jax.random.fold_in(key, 3), rows)[jnp.arange(count) % rows]
    chance = jnp.where(jnp.arange(rows)[:, None] == fixed_rows[None, :], 1 << 14, chance)
    score = chance * count + jnp.arange(count)
    return lax.top_k(score.astype(jnp.int32), top)[1].astype(jnp.int32)


def gaussian(stream_key, dims, scale, most, cuts=(), kind=jnp.bfloat16):
    values = scale * jax.random.normal(stream_key, dims, jnp.float32)
    if cuts:
        values = values * block_scale(stream_key, dims, cuts, -0.22, 0.18)
    return jnp.clip(values, -most, most).astype(kind)


def setup_inputs(seed: int = 0) -> dict:
    splits = jax.random.split(jax.random.key(seed), 9)
    return {
        "leaf_rhs": gaussian(splits[0], (NBLK, W, NS), 1.0, 6.0, ((0, 8), (2, 16)), jnp.float32),
        "top_rhs": gaussian(splits[1], (S, NS), 1.0, 6.0, ((1, 16),), jnp.float32),
        "leaf_inv": draw_leaf_inv(jax.random.fold_in(splits[8], 71), 0),
        "coupling": gaussian(splits[3], (NBLK, S, W), (NBLK * W) ** -0.5, 0.046875, ((0, 8),), jnp.float32),
        "top_inv": draw_top_inv(jax.random.fold_in(splits[8], 71), 0),
        "cond": jnp.clip(jnp.exp(math.log(3.0) - 3.4011974 * jax.random.uniform(splits[5], (NBLK, W), jnp.float32) ** block_scale(splits[5], (NBLK, W), ((0, 8),), -0.2, 0.2)), 0.1, 3.0),
        "electrodes": picks_of(splits[6], NQ, NS, 4, 0),
        "blocks": set_ends(ranked_ids(splits[7], (KB, NQ), NBLK, 2), jax.random.fold_in(splits[7], 3), 0, NBLK - 1).astype(jnp.int32),
    }


def reference(leaf_rhs, top_rhs, leaf_inv, coupling, top_inv, cond, electrodes, blocks):
    highest = lax.Precision.HIGHEST
    forward_leaf = jnp.einsum("bij,bjs->bis", leaf_inv, leaf_rhs, precision=highest)
    coupled = jnp.einsum("bti,bis->ts", coupling, forward_leaf, precision=highest)
    residual = top_rhs - coupled
    forward_top = jnp.dot(top_inv, residual, precision=highest)
    separator_field = jnp.dot(top_inv.T, forward_top, precision=highest)
    adjusted = forward_leaf - jnp.einsum("bti,ts->bis", coupling, separator_field, precision=highest)
    leaf_field = jnp.einsum("bji,bjs->bis", leaf_inv, adjusted, precision=highest)
    cell_ids = jnp.arange(W, dtype=jnp.int32)

    def block_row(block_ids):
        def difference(plus_ids, minus_ids):
            upper = leaf_field[block_ids[None, :], cell_ids[:, None], plus_ids[None, :]]
            lower = leaf_field[block_ids[None, :], cell_ids[:, None], minus_ids[None, :]]
            return upper - lower

        current = difference(electrodes[:, 0], electrodes[:, 1])
        potential = difference(electrodes[:, 2], electrodes[:, 3])
        weight = cond[block_ids].T
        return weight * (current * potential)

    return lax.map(block_row, blocks)
```

```python
import jax
import jax.numpy as jnp
import numpy as np
from jax import lax
from jax.experimental import pallas as pl
from jax.experimental.pallas import tpu as pltpu
from jax.sharding import Mesh, PartitionSpec as P

HIGH = lax.Precision.HIGH
HIGHEST = lax.Precision.HIGHEST
UNROLL = 32
CHIPS = 64


def leaf_kernel(inv_ref, adjusted_ref, cond_ref, out_ref):
    for j in range(8):
        field = lax.dot_general(
            inv_ref[j], adjusted_ref[j], (((0,), (0,)), ((), ())),
            precision=HIGHEST, preferred_element_type=jnp.float32,
        )
        weight = jnp.sqrt(cond_ref[j : j + 1, :])
        field = field * jnp.broadcast_to(weight, (128, 256)).T
        for c4 in range(4):
            row = (c4 // 2) * 16 + j * 2 + c4 % 2
            out_ref[pl.ds(row, CHIPS, stride=32), :] = field[c4 * CHIPS : (c4 + 1) * CHIPS, :]


def leaf_send(inv, adjusted, cond):
    return pl.pallas_call(
        leaf_kernel,
        out_shape=jax.ShapeDtypeStruct((CHIPS * 32, 128), jnp.float32),
        compiler_params=pltpu.CompilerParams(vmem_limit_bytes=32 << 20),
        name="leaf_send",
    )(inv, adjusted, cond)


def select_kernel(el_ref, bl_ref, even_ref, odd_ref, out_ref, rows_ref, prod_ref):
    @pl.when(pl.program_id(0) == 0)
    def _():
        for chip in range(8):
            for core, ref in enumerate((even_ref, odd_ref)):
                for half in range(2):
                    parts = [ref[chip, p * 32 + half * 16 : p * 32 + half * 16 + 16, :] for p in range(8)]
                    at = (chip * 2 + core) * 128
                    rows_ref[at : at + 128, half, :] = jnp.concatenate(parts, axis=0).T

    quads_n = prod_ref.shape[0] // 2

    def body(group, carry):
        base = pl.multiple_of(group * UNROLL, UNROLL)
        for step in range(UNROLL):
            q = base + step
            a = rows_ref[el_ref[q]]
            b = rows_ref[el_ref[quads_n + q]]
            c = rows_ref[el_ref[2 * quads_n + q]]
            d = rows_ref[el_ref[3 * quads_n + q]]
            prod_ref[pl.ds(2 * base + 2 * step, 2), :] = (a - b) * (c - d)
        return carry

    lax.fori_loop(0, quads_n // UNROLL, body, 0)
    for t in range(quads_n // 128):
        lanes = bl_ref[0, :, t * 128 : (t + 1) * 128] * 2
        ids = jnp.concatenate([lanes, lanes + 1, jnp.zeros((96, 128), jnp.int32)], axis=0).T
        for half in range(2):
            prod = prod_ref[pl.ds(t * 256 + half, 128, stride=2), :]
            sel = jnp.take_along_axis(prod, ids, axis=1).T
            for p in range(8):
                for c2 in range(2):
                    at = c2 * 16 + 2 * p
                    to = t * 8 + (half * 2 + c2) * 2
                    out_ref[p, to : to + 2, :] = sel[at : at + 2, :]


def select(el, bl, even, odd):
    return pl.pallas_call(
        select_kernel,
        grid=(8,),
        out_shape=jax.ShapeDtypeStruct((CHIPS, 32, 128), jnp.float32),
        in_specs=[
            pl.BlockSpec((2048,), lambda i: (i,), memory_space=pltpu.SMEM),
            pl.BlockSpec((1, 16, 512), lambda i: (i, 0, 0)),
            pl.BlockSpec((8, 256, 128), lambda i: (0, 0, 0)),
            pl.BlockSpec((8, 256, 128), lambda i: (0, 0, 0)),
        ],
        out_specs=pl.BlockSpec((8, 32, 128), lambda i: (i, 0, 0)),
        scratch_shapes=[
            pltpu.VMEM((2048, 2, 128), jnp.float32),
            pltpu.VMEM((1024, 128), jnp.float32),
        ],
        compiler_params=pltpu.CompilerParams(vmem_limit_bytes=32 << 20),
        name="select_quads",
    )(el, bl, even, odd)


def assemble_kernel(in_ref, out_ref):
    for t in range(4):
        for c4 in range(4):
            for k2 in range(2):
                out_ref[k2, c4 * CHIPS : (c4 + 1) * CHIPS, t * 128 : (t + 1) * 128] = in_ref[
                    pl.ds(t * 8 + c4 * 2 + k2, CHIPS, stride=32), :
                ]


def assemble(received):
    return pl.pallas_call(
        assemble_kernel,
        out_shape=jax.ShapeDtypeStruct((2, 256, 512), jnp.float32),
        name="assemble_sens",
    )(received)


def reduce_scatter(value, rows):
    parts = lax.all_to_all(value.reshape(8, rows, -1), "snode", 0, 0, tiled=True)
    return jnp.sum(parts, axis=0)


def all_gather(block):
    whole = jnp.broadcast_to(block[None], (8,) + block.shape)
    return lax.all_to_all(whole, "snode", 0, 0, tiled=True).reshape(8 * block.shape[0], -1)


def local(leaf_rhs, top_rhs, leaf_inv, coupling, top_inv, cond, electrodes, blocks):
    me = lax.axis_index("snode")

    lists = jnp.concatenate([electrodes.T, blocks, jnp.zeros((12, 512), jnp.int32)], axis=0)
    lists = lax.all_gather(lists.astype(jnp.float32).reshape(128, 128), ("chip", "core"), axis=0, tiled=True)
    lists = lists.reshape(8, 2, 32, 512)
    lists = lax.dynamic_index_in_dim(lists, lax.axis_index("core"), 1, keepdims=False).astype(jnp.int32)
    el = lists[:, :4].reshape(8 * 2048)
    bl = lists[:, 4:20]

    forward_leaf = jnp.einsum("bij,bjs->bis", leaf_inv, leaf_rhs, precision=HIGH)
    partial_value = jnp.einsum("bti,bis->ts", coupling, forward_leaf, precision=HIGH)
    coupled = reduce_scatter(partial_value, 256)
    residual = lax.dynamic_slice_in_dim(top_rhs, me * 256, 256, 0) - coupled
    residual = all_gather(residual)
    forward_top = jnp.dot(top_inv, residual, precision=HIGH)
    top_partial = jnp.einsum("rt,rs->ts", top_inv, forward_top, precision=HIGH)
    separator_field = all_gather(reduce_scatter(top_partial, 256))
    adjusted = forward_leaf - jnp.einsum("bti,ts->bis", coupling, separator_field, precision=HIGH)

    send = leaf_send(leaf_inv, adjusted, cond)
    own = lax.all_to_all(send.reshape(CHIPS, 32, 128), ("chip", "snode"), 0, 0, tiled=True)
    own = own.reshape(8, 256, 128)
    other = lax.ppermute(own, "core", [(0, 1), (1, 0)])
    odd = lax.axis_index("core") == 1
    picked = select(el, bl, jnp.where(odd, other, own), jnp.where(odd, own, other))
    received = lax.all_to_all(picked, ("chip", "snode"), 0, 0, tiled=True)
    return assemble(received.reshape(CHIPS * 32, 128))


def solution(mesh):
    devices = np.asarray(mesh.devices)
    fine = Mesh(devices.reshape(8, 2, 8), ("chip", "core", "snode"))
    src = ("chip", "core")
    return jax.shard_map(
        local,
        mesh=fine,
        in_specs=(
            P("snode", None, src),
            P(None, src),
            P("snode", None, None),
            P("snode", None, None),
            P("snode", None),
            P("snode", None),
            P(src, None),
            P(None, src),
        ),
        out_specs=P("snode", None, src),
        check_vma=False,
    )
```

```python
import jax
import jax.numpy as jnp
import numpy as np
from jax import lax
from jax.experimental import pallas as pl
from jax.experimental.pallas import tpu as pltpu
from jax.sharding import Mesh, PartitionSpec as P

UNROLL = 64
CHIPS = 64


def two(value):
    high = value.astype(jnp.bfloat16)
    return high, (value - high.astype(jnp.float32)).astype(jnp.bfloat16)


def mm(a, b):
    return jnp.dot(a, b, preferred_element_type=jnp.float32)


def params():
    return pltpu.CompilerParams(vmem_limit_bytes=40 << 20)


def front_kernel(inv_ref, rhs_ref, coupling_ref, sum_ref, forward_ref):
    j = pl.program_id(0)

    @pl.when(j == 0)
    def _():
        sum_ref[...] = jnp.zeros_like(sum_ref)

    ih, il = two(inv_ref[0])
    rh, rl = two(rhs_ref[0])
    both = jnp.concatenate([rh, rl], axis=1)
    wide = mm(ih, both)
    last = mm(il, both)
    forward = wide[:, :128] + (wide[:, 128:] + (last[:, :128] + last[:, 128:]))
    forward_ref[0] = forward.T
    fh, fl = two(forward)
    both = jnp.concatenate([fh, fl], axis=1)
    for r in range(0, coupling_ref.shape[1], 512):
        ch, cl = two(coupling_ref[0, r : r + 512, :])
        wide = mm(ch, both)
        sum_ref[r : r + 512, :] += wide[:, :128] + wide[:, 128:] + mm(cl, fh)


def front(inv, rhs, coupling):
    return pl.pallas_call(
        front_kernel,
        grid=(8,),
        out_shape=(
            jax.ShapeDtypeStruct((2048, 128), jnp.float32),
            jax.ShapeDtypeStruct((8, 128, 256), jnp.float32),
        ),
        in_specs=[
            pl.BlockSpec((1, 256, 256), lambda j: (j, 0, 0)),
            pl.BlockSpec((1, 256, 128), lambda j: (j, 0, 0)),
            pl.BlockSpec((1, 2048, 256), lambda j: (j, 0, 0)),
        ],
        out_specs=(
            pl.BlockSpec((2048, 128), lambda j: (0, 0)),
            pl.BlockSpec((1, 128, 256), lambda j: (j, 0, 0)),
        ),
        compiler_params=params(),
        name="leaf_front",
    )(inv, rhs, coupling)


def residual_kernel(me_ref, parts_ref, top_ref, out_ref):
    value = top_ref[...]
    for p in range(8):
        value = value - parts_ref[p]
    for p in range(8):
        out_ref[p] = value


def residual(me, parts, top):
    return pl.pallas_call(
        residual_kernel,
        grid_spec=pltpu.PrefetchScalarGridSpec(
            num_scalar_prefetch=1,
            grid=(1,),
            in_specs=[
                pl.BlockSpec((8, 256, 128), lambda i, me: (0, 0, 0)),
                pl.BlockSpec((256, 128), lambda i, me: (me[0], 0)),
            ],
            out_specs=pl.BlockSpec((8, 256, 128), lambda i, me: (0, 0, 0)),
        ),
        out_shape=jax.ShapeDtypeStruct((8, 256, 128), jnp.float32),
        compiler_params=params(),
        name="residual",
    )(me, parts, top)


def spread_kernel(parts_ref, out_ref):
    value = parts_ref[0]
    for p in range(1, 8):
        value = value + parts_ref[p]
    for p in range(8):
        out_ref[p] = value


def spread(parts):
    return pl.pallas_call(
        spread_kernel,
        out_shape=jax.ShapeDtypeStruct(parts.shape, jnp.float32),
        compiler_params=params(),
        name="spread",
    )(parts)


def top_kernel(inv_ref, res_ref, out_ref):
    total = None
    for p in range(8):
        th, tl = two(inv_ref[:, p * 256 : (p + 1) * 256])
        rh, rl = two(res_ref[p])
        wide = mm(th, jnp.concatenate([rh, rl], axis=1))
        term = wide[:, :128] + wide[:, 128:] + mm(tl, rh)
        total = term if total is None else total + term
    fh, fl = two(total.T)
    both = jnp.concatenate([fh, fl], axis=0)
    for p in range(8):
        th, tl = two(inv_ref[:, p * 256 : (p + 1) * 256])
        wide = mm(both, th)
        out_ref[p] = wide[:128] + wide[128:] + mm(fh, tl)


def top(inv, res):
    return pl.pallas_call(
        top_kernel,
        out_shape=jax.ShapeDtypeStruct((8, 128, 256), jnp.float32),
        compiler_params=params(),
        name="top_solve",
    )(inv, res)


def back_kernel(sep_ref, forward_ref, coupling_ref, inv_ref, cond_ref, out_ref, split_ref, total_ref):
    j = pl.program_id(0)

    @pl.when(j == 0)
    def _():
        for p in range(8):
            split_ref[p, :128], split_ref[p, 128:] = two(sep_ref[p])

    total = forward_ref[0]
    for p in range(8):
        ch, cl = two(coupling_ref[0, p * 256 : (p + 1) * 256, :])
        wide = mm(split_ref[p], ch)
        total = total - (wide[:128] + wide[128:] + mm(split_ref[p, :128], cl))
    total_ref[j] = total

    @pl.when(j == 7)
    def _():
        for b in range(8):
            th, tl = two(total_ref[b])
            ih, il = two(inv_ref[b])
            both = jnp.concatenate([th, tl], axis=0)
            wide = mm(both, ih)
            last = mm(both, il)
            field = wide[:128] + (wide[128:] + (last[:128] + last[128:]))
            field = (field * jnp.sqrt(cond_ref[b : b + 1, :])).T
            for c4 in range(4):
                row = (c4 // 2) * 16 + b * 2 + c4 % 2
                out_ref[pl.ds(row, CHIPS, stride=32), :] = field[c4 * CHIPS : (c4 + 1) * CHIPS, :]


def back(sep, forward, coupling, inv, cond):
    return pl.pallas_call(
        back_kernel,
        grid=(8,),
        out_shape=jax.ShapeDtypeStruct((CHIPS * 32, 128), jnp.float32),
        in_specs=[
            pl.BlockSpec((8, 128, 256), lambda j: (0, 0, 0)),
            pl.BlockSpec((1, 128, 256), lambda j: (j, 0, 0)),
            pl.BlockSpec((1, 2048, 256), lambda j: (j, 0, 0)),
            pl.BlockSpec((8, 256, 256), lambda j: (0, 0, 0)),
            pl.BlockSpec((8, 256), lambda j: (0, 0)),
        ],
        out_specs=pl.BlockSpec((CHIPS * 32, 128), lambda j: (0, 0)),
        scratch_shapes=[
            pltpu.VMEM((8, 256, 256), jnp.bfloat16),
            pltpu.VMEM((8, 128, 256), jnp.float32),
        ],
        compiler_params=params(),
        name="leaf_back",
    )(sep, forward, coupling, inv, cond)


def select_kernel(core_ref, el_ref, lists_ref, own_ref, other_ref, out_ref, rows_ref, prod_ref, ids_ref):
    @pl.when(pl.program_id(0) == 0)
    def _():
        for chip in range(8):
            for ref, core in ((own_ref, core_ref[0]), (other_ref, 1 - core_ref[0])):
                for half in range(2):
                    parts = [ref[chip, p * 32 + half * 16 : p * 32 + half * 16 + 16, :] for p in range(8)]
                    at = (chip * 2 + core) * 256 + half
                    rows_ref[pl.ds(at, 128, stride=2), :] = jnp.concatenate(parts, axis=0).T

    quads_n = prod_ref.shape[0] // 2

    def field(at):
        return rows_ref[pl.ds(pl.multiple_of(el_ref[at], 2), 2), :]

    def body(group, carry):
        base = pl.multiple_of(group * UNROLL, UNROLL)
        for step in range(UNROLL):
            q = base + step
            a = field(q)
            b = field(quads_n + q)
            c = field(2 * quads_n + q)
            d = field(3 * quads_n + q)
            prod_ref[pl.ds(2 * base + 2 * step, 2), :] = (a - b) * (c - d)
        return carry

    lax.fori_loop(0, quads_n // UNROLL, body, 0)

    lane = lax.broadcasted_iota(jnp.int32, (128, 128), 1)
    second = lane & 8 != 0
    upper = lane & 4 != 0
    for pair in range(2):
        for t2 in range(2):
            for k2 in range(2):
                at = 16 + k2 * 4 + pair * 2 + t2
                lanes = lists_ref[pl.ds(at, 8, stride=8), :].astype(jnp.int32) * 2
                for c2 in range(2):
                    for half in range(2):
                        ids_ref[pl.ds(t2 * 8 + half * 4 + c2 * 2 + k2, 8, stride=16), :] = lanes + c2
        ids = ids_ref[...].T
        tiles = []
        for t2 in range(2):
            for half in range(2):
                prod = prod_ref[pl.ds((pair * 2 + t2) * 256 + half, 128, stride=2), :]
                tiles.append(jnp.take_along_axis(prod, ids, axis=1))
        low = jnp.where(upper, tiles[1], tiles[0])
        high = jnp.where(upper, tiles[3], tiles[2])
        sel = jnp.where(second, high, low).T
        for p in range(8):
            out_ref[p, pair * 16 : (pair + 1) * 16, :] = sel[p * 16 : (p + 1) * 16, :]


def select(core, el, lists, own, other):
    return pl.pallas_call(
        select_kernel,
        grid_spec=pltpu.PrefetchScalarGridSpec(
            num_scalar_prefetch=1,
            grid=(8,),
            in_specs=[
                pl.BlockSpec((2048,), lambda i, core: (i,), memory_space=pltpu.SMEM),
                pl.BlockSpec((128, 128), lambda i, core: (2 * i + core[0], 0)),
                pl.BlockSpec((8, 256, 128), lambda i, core: (0, 0, 0)),
                pl.BlockSpec((8, 256, 128), lambda i, core: (0, 0, 0)),
            ],
            out_specs=pl.BlockSpec((8, 32, 128), lambda i, core: (i, 0, 0)),
            scratch_shapes=[
                pltpu.VMEM((4096, 128), jnp.float32),
                pltpu.VMEM((1024, 128), jnp.float32),
                pltpu.VMEM((128, 128), jnp.int32),
            ],
        ),
        out_shape=jax.ShapeDtypeStruct((CHIPS, 32, 128), jnp.float32),
        compiler_params=params(),
        name="select_quads",
    )(core, el, lists, own, other)


def assemble_kernel(in_ref, out_ref):
    n = out_ref.shape[2]
    for t in range(4):
        for c4 in range(4):
            for k2 in range(2):
                out_ref[k2, c4, :, t * 128 : (t + 1) * 128] = in_ref[
                    pl.ds(t * 8 + c4 * 2 + k2, n, stride=32), :
                ]


def assemble(received):
    out = pl.pallas_call(
        assemble_kernel,
        grid=(4,),
        out_shape=jax.ShapeDtypeStruct((2, 4, CHIPS, 512), jnp.float32),
        in_specs=[pl.BlockSpec((512, 128), lambda i: (i, 0))],
        out_specs=pl.BlockSpec((2, 4, 16, 512), lambda i: (0, 0, i, 0)),
        compiler_params=params(),
        name="assemble_sens",
    )(received)
    return out.reshape(2, 256, 512)

def exchange(parts):
    return lax.all_to_all(parts, "snode", 0, 0, tiled=True)


def local(leaf_rhs, top_rhs, leaf_inv, coupling, top_inv, cond, electrodes, blocks):
    me = lax.axis_index("snode").astype(jnp.int32).reshape(1)
    core = lax.axis_index("core").astype(jnp.int32).reshape(1)

    lists = [(electrodes.T * 2).reshape(16, 128), blocks.reshape(64, 128), jnp.zeros((48, 128), jnp.int32)]
    lists = jnp.concatenate(lists, axis=0).astype(jnp.float32)
    lists = lax.all_gather(lists, ("chip", "core"), axis=0, tiled=True)
    el = lists.reshape(8, 2, 128, 128)[:, :, :16]
    el = jnp.where(core[0] == 1, el[:, 1], el[:, 0]).astype(jnp.int32).reshape(8 * 2048)

    partial_value, forward = front(leaf_inv, leaf_rhs, coupling)
    coupled = exchange(partial_value.reshape(8, 256, 128))
    res = exchange(residual(me, coupled, top_rhs))
    separator = exchange(spread(exchange(top(top_inv, res))))

    send = back(separator, forward, coupling, leaf_inv, cond)
    own = lax.all_to_all(send.reshape(CHIPS, 32, 128), ("chip", "snode"), 0, 0, tiled=True)
    own = own.reshape(8, 256, 128)
    other = lax.ppermute(own, "core", [(0, 1), (1, 0)])
    picked = select(core, el, lists, own, other)
    received = lax.all_to_all(picked, ("chip", "snode"), 0, 0, tiled=True)
    return assemble(received.reshape(CHIPS * 32, 128))


def solution(mesh):
    devices = np.asarray(mesh.devices)
    fine = Mesh(devices.reshape(8, 2, 8), ("chip", "core", "snode"))
    src = ("chip", "core")
    return jax.shard_map(
        local,
        mesh=fine,
        in_specs=(
            P("snode", None, src),
            P(None, src),
            P("snode", None, None),
            P("snode", None, None),
            P("snode", None),
            P("snode", None),
            P(src, None),
            P(None, src),
        ),
        out_specs=P("snode", None, src),
        check_vma=False,
    )
```

```python
import jax
import jax.numpy as jnp
import numpy as np
from jax import lax
from jax.experimental import pallas as pl
from jax.experimental.pallas import tpu as pltpu
from jax.sharding import Mesh, PartitionSpec as P

UNROLL = 64
CHIPS = 64


def two(value):
    high = value.astype(jnp.bfloat16)
    return high, (value - high.astype(jnp.float32)).astype(jnp.bfloat16)


def mm(a, b):
    return jnp.dot(a, b, preferred_element_type=jnp.float32)


def params(mib):
    return pltpu.CompilerParams(vmem_limit_bytes=mib << 20)


PANEL = jax.ShapeDtypeStruct((256, 128), jnp.float32)


def front_kernel(inv_ref, rhs_ref, coupling_ref, sum_ref, forward_ref):
    j = pl.program_id(0)

    @pl.when(j == 0)
    def _():
        sum_ref[...] = jnp.zeros_like(sum_ref)

    ih, il = two(inv_ref[0])
    rh, rl = two(rhs_ref[0])
    both = jnp.concatenate([rh, rl], axis=1)
    wide = mm(ih, both)
    last = mm(il, both)
    forward = wide[:, :128] + (wide[:, 128:] + (last[:, :128] + last[:, 128:]))
    forward_ref[0] = forward.T
    fh, fl = two(forward)
    both = jnp.concatenate([fh, fl], axis=1)
    for r in range(0, coupling_ref.shape[1], 512):
        ch, cl = two(coupling_ref[0, r : r + 512, :])
        wide = mm(ch, both)
        sum_ref[r : r + 512, :] += wide[:, :128] + wide[:, 128:] + mm(cl, fh)


def front(inv, rhs, coupling):
    return pl.pallas_call(
        front_kernel,
        grid=(8,),
        out_shape=(
            jax.ShapeDtypeStruct((2048, 128), jnp.float32),
            jax.ShapeDtypeStruct((8, 128, 256), jnp.float32),
        ),
        in_specs=[
            pl.BlockSpec((1, 256, 256), lambda j: (j, 0, 0)),
            pl.BlockSpec((1, 256, 128), lambda j: (j, 0, 0)),
            pl.BlockSpec((1, 2048, 256), lambda j: (j, 0, 0)),
        ],
        out_specs=(
            pl.BlockSpec((2048, 128), lambda j: (0, 0)),
            pl.BlockSpec((1, 128, 256), lambda j: (j, 0, 0)),
        ),
        compiler_params=params(60),
        name="leaf_front",
    )(inv, rhs, coupling)


def residual_kernel(top_ref, parts_ref, out_ref):
    value = top_ref[...]
    for p in range(8):
        value = value - parts_ref[p]
    out_ref[...] = value


def residual(top, parts):
    return pl.pallas_call(
        residual_kernel,
        out_shape=PANEL,
        compiler_params=params(16),
        name="residual",
    )(top, parts)


def total_kernel(parts_ref, out_ref):
    value = parts_ref[0]
    for p in range(1, 8):
        value = value + parts_ref[p]
    out_ref[...] = value


def total(parts):
    return pl.pallas_call(
        total_kernel,
        out_shape=jax.ShapeDtypeStruct((128, 256), jnp.float32),
        compiler_params=params(16),
        name="separator",
    )(parts)


def top_kernel(me_ref, inv_ref, *refs):
    res, out_ref = refs[:8], refs[8]
    total = None
    for d in range(8):
        p = (me_ref[0] ^ (d // 2)) * 2 + (me_ref[1] ^ (d % 2))
        th, tl = two(inv_ref[:, pl.ds(pl.multiple_of(p * 256, 256), 256)])
        rh, rl = two(res[d][...])
        wide = mm(th, jnp.concatenate([rh, rl], axis=1))
        term = wide[:, :128] + wide[:, 128:] + mm(tl, rh)
        total = term if total is None else total + term
    fh, fl = two(total.T)
    both = jnp.concatenate([fh, fl], axis=0)
    for p in range(8):
        th, tl = two(inv_ref[:, p * 256 : (p + 1) * 256])
        wide = mm(both, th)
        out_ref[p] = wide[:128] + wide[128:] + mm(fh, tl)


def top(me, inv, res):
    return pl.pallas_call(
        top_kernel,
        grid_spec=pltpu.PrefetchScalarGridSpec(
            num_scalar_prefetch=1,
            grid=(1,),
            in_specs=[pl.BlockSpec((256, 2048), lambda i, me: (0, 0))]
            + [pl.BlockSpec((256, 128), lambda i, me: (0, 0))] * 8,
            out_specs=pl.BlockSpec((8, 128, 256), lambda i, me: (0, 0, 0)),
        ),
        out_shape=jax.ShapeDtypeStruct((8, 128, 256), jnp.float32),
        compiler_params=params(24),
        name="top_solve",
    )(me, inv, *res)


def back_kernel(me_ref, *refs):
    sep, (forward_ref, coupling_ref, inv_ref, cond_ref, out_ref, split_ref, total_ref) = refs[:8], refs[8:]
    j = pl.program_id(0)

    @pl.when(j == 0)
    def _():
        for d in range(8):
            p = (me_ref[0] ^ (d // 2)) * 2 + (me_ref[1] ^ (d % 2))
            split_ref[p, :128], split_ref[p, 128:] = two(sep[d][...])

    total = forward_ref[0]
    for p in range(8):
        ch, cl = two(coupling_ref[0, p * 256 : (p + 1) * 256, :])
        wide = mm(split_ref[p], ch)
        total = total - (wide[:128] + wide[128:] + mm(split_ref[p, :128], cl))
    total_ref[j] = total

    @pl.when(j == 7)
    def _():
        for b in range(8):
            th, tl = two(total_ref[b])
            ih, il = two(inv_ref[b])
            both = jnp.concatenate([th, tl], axis=0)
            wide = mm(both, ih)
            last = mm(both, il)
            field = wide[:128] + (wide[128:] + (last[:128] + last[128:]))
            field = (field * jnp.sqrt(cond_ref[b : b + 1, :])).T
            for c4 in range(4):
                row = (c4 // 2) * 16 + b * 2 + c4 % 2
                out_ref[pl.ds(row, CHIPS, stride=32), :] = field[c4 * CHIPS : (c4 + 1) * CHIPS, :]


def back(me, sep, forward, coupling, inv, cond):
    return pl.pallas_call(
        back_kernel,
        grid_spec=pltpu.PrefetchScalarGridSpec(
            num_scalar_prefetch=1,
            grid=(8,),
            in_specs=[pl.BlockSpec((128, 256), lambda j, me: (0, 0))] * 8
            + [
                pl.BlockSpec((1, 128, 256), lambda j, me: (j, 0, 0)),
                pl.BlockSpec((1, 2048, 256), lambda j, me: (j, 0, 0)),
                pl.BlockSpec((8, 256, 256), lambda j, me: (0, 0, 0)),
                pl.BlockSpec((8, 256), lambda j, me: (0, 0)),
            ],
            out_specs=pl.BlockSpec((CHIPS * 32, 128), lambda j, me: (0, 0)),
            scratch_shapes=[
                pltpu.VMEM((8, 256, 256), jnp.bfloat16),
                pltpu.VMEM((8, 128, 256), jnp.float32),
            ],
        ),
        out_shape=jax.ShapeDtypeStruct((CHIPS * 32, 128), jnp.float32),
        compiler_params=params(48),
        name="leaf_back",
    )(me, *sep, forward, coupling, inv, cond)


def select_kernel(core_ref, el_ref, lists_ref, own_ref, other_ref, out_ref, rows_ref, prod_ref, ids_ref, lanes_ref):
    @pl.when(pl.program_id(0) == 0)
    def _():
        for chip in range(8):
            for ref, core in ((own_ref, core_ref[0]), (other_ref, 1 - core_ref[0])):
                for half in range(2):
                    parts = [ref[chip, p * 32 + half * 16 : p * 32 + half * 16 + 16, :] for p in range(8)]
                    at = (chip * 2 + core) * 256 + half
                    rows_ref[pl.ds(at, 128, stride=2), :] = jnp.concatenate(parts, axis=0).T

    quads_n = prod_ref.shape[0] // 2

    def field(at):
        return rows_ref[pl.ds(pl.multiple_of(el_ref[at], 2), 2), :]

    def body(group, carry):
        base = pl.multiple_of(group * UNROLL, UNROLL)
        for step in range(UNROLL):
            q = base + step
            a = field(q)
            b = field(quads_n + q)
            c = field(2 * quads_n + q)
            d = field(3 * quads_n + q)
            prod_ref[pl.ds(2 * base + 2 * step, 2), :] = (a - b) * (c - d)
        return carry

    lax.fori_loop(0, quads_n // UNROLL, body, 0)

    lane = lax.broadcasted_iota(jnp.int32, (128, 128), 1)
    second = lane & 8 != 0
    upper = lane & 4 != 0
    for pair in range(2):
        for t2 in range(2):
            at = (pair * 2 + t2) * 128
            lanes_ref[...] = lists_ref[:16, at : at + 128].astype(jnp.int32) * 2
            for k2 in range(2):
                lanes = lanes_ref[pl.ds(k2, 8, stride=2), :]
                for c2 in range(2):
                    for half in range(2):
                        ids_ref[pl.ds(t2 * 8 + half * 4 + c2 * 2 + k2, 8, stride=16), :] = lanes + c2
        ids = ids_ref[...].T
        tiles = []
        for t2 in range(2):
            for half in range(2):
                prod = prod_ref[pl.ds((pair * 2 + t2) * 256 + half, 128, stride=2), :]
                tiles.append(jnp.take_along_axis(prod, ids, axis=1))
        low = jnp.where(upper, tiles[1], tiles[0])
        high = jnp.where(upper, tiles[3], tiles[2])
        sel = jnp.where(second, high, low).T
        for p in range(8):
            out_ref[p, pair * 16 : (pair + 1) * 16, :] = sel[p * 16 : (p + 1) * 16, :]


def select(core, el, lists, own, other):
    return pl.pallas_call(
        select_kernel,
        grid_spec=pltpu.PrefetchScalarGridSpec(
            num_scalar_prefetch=1,
            grid=(8,),
            in_specs=[
                pl.BlockSpec((2048,), lambda i, core: (i,), memory_space=pltpu.SMEM),
                pl.BlockSpec((32, 512), lambda i, core: (2 * i + core[0], 0)),
                pl.BlockSpec((8, 256, 128), lambda i, core: (0, 0, 0)),
                pl.BlockSpec((8, 256, 128), lambda i, core: (0, 0, 0)),
            ],
            out_specs=pl.BlockSpec((8, 32, 128), lambda i, core: (i, 0, 0)),
            scratch_shapes=[
                pltpu.VMEM((4096, 128), jnp.float32),
                pltpu.VMEM((1024, 128), jnp.float32),
                pltpu.VMEM((128, 128), jnp.int32),
                pltpu.VMEM((16, 128), jnp.int32),
            ],
        ),
        out_shape=jax.ShapeDtypeStruct((CHIPS, 32, 128), jnp.float32),
        compiler_params=params(24),
        name="select_quads",
    )(core, el, lists, own, other)


def assemble_kernel(in_ref, out_ref):
    n = out_ref.shape[2]
    for t in range(4):
        for c4 in range(4):
            for k2 in range(2):
                out_ref[k2, c4, :, t * 128 : (t + 1) * 128] = in_ref[
                    pl.ds(t * 8 + c4 * 2 + k2, n, stride=32), :
                ]


def assemble(received):
    out = pl.pallas_call(
        assemble_kernel,
        grid=(4,),
        out_shape=jax.ShapeDtypeStruct((2, 4, CHIPS, 512), jnp.float32),
        in_specs=[pl.BlockSpec((512, 128), lambda i: (i, 0))],
        out_specs=pl.BlockSpec((2, 4, 16, 512), lambda i: (0, 0, i, 0)),
        compiler_params=params(16),
        name="assemble_sens",
    )(received)
    return out.reshape(2, 256, 512)

def exchange(parts):
    return lax.all_to_all(parts, ("y", "z"), 0, 0, tiled=True)


def send(value, d):
    return lax.ppermute(value, ("y", "z"), [(i, i ^ d) for i in range(8)])


def swap(value, axis):
    return lax.ppermute(value, axis, [(0, 1), (1, 0)])


def all_panels(own):
    far = swap(own, "z")
    return [send(value, 2 * dy) if dy else value for dy in range(4) for value in (own, far)]


def local(leaf_rhs, top_rhs, leaf_inv, coupling, top_inv, cond, electrodes, blocks):
    me = jnp.stack([lax.axis_index("y"), lax.axis_index("z")]).astype(jnp.int32)
    core = lax.axis_index("core").astype(jnp.int32).reshape(1)

    partial_value, forward = front(leaf_inv, leaf_rhs, coupling)
    electrodes, blocks, partial_value = lax.optimization_barrier((electrodes, blocks, partial_value))
    lists = [blocks, electrodes.T * 2, jnp.zeros((12, 512), jnp.int32)]
    lists = jnp.concatenate(lists, axis=0).astype(jnp.float32)
    lists = lax.all_gather(lists, ("chip", "core"), axis=0, tiled=True)
    el = lists.reshape(8, 2, 32, 512)[:, :, 16:20]
    el = jnp.where(core[0] == 1, el[:, 1], el[:, 0]).astype(jnp.int32).reshape(8 * 2048)

    at = (me[0] * 2 + me[1]) * 256
    top_own = lax.dynamic_slice_in_dim(top_rhs, at, 256, 0)
    res = residual(top_own, exchange(partial_value.reshape(8, 256, 128)))
    separator = all_panels(total(exchange(top(me, top_inv, all_panels(res)))))
    separator, el, lists = lax.optimization_barrier((separator, el, lists))

    fields = back(me, separator, forward, coupling, leaf_inv, cond)
    own = lax.all_to_all(fields.reshape(CHIPS, 32, 128), ("chip", "y", "z"), 0, 0, tiled=True)
    own = own.reshape(8, 256, 128)
    other = lax.ppermute(own, "core", [(0, 1), (1, 0)])
    picked = select(core, el, lists, own, other)
    received = lax.all_to_all(picked, ("chip", "y", "z"), 0, 0, tiled=True)
    return assemble(received.reshape(CHIPS * 32, 128))


def solution(mesh):
    devices = np.asarray(mesh.devices)
    fine = Mesh(devices.reshape(8, 2, 4, 2), ("chip", "core", "y", "z"))
    src = ("chip", "core")
    snode = ("y", "z")
    return jax.shard_map(
        local,
        mesh=fine,
        in_specs=(
            P(snode, None, src),
            P(None, src),
            P(snode, None, None),
            P(snode, None, None),
            P(snode, None),
            P(snode, None),
            P(src, None),
            P(None, src),
        ),
        out_specs=P(snode, None, src),
        check_vma=False,
    )
```

```python
import jax
import jax.numpy as jnp
import numpy as np
from jax import lax
from jax.experimental import pallas as pl
from jax.experimental.pallas import tpu as pltpu
from jax.sharding import Mesh, PartitionSpec as P

CHIPS = 64


def two(value):
    high = value.astype(jnp.bfloat16)
    return high, (value - high.astype(jnp.float32)).astype(jnp.bfloat16)


def mm(a, b):
    return jnp.dot(a, b, preferred_element_type=jnp.float32)


def params(mib):
    return pltpu.CompilerParams(vmem_limit_bytes=mib << 20)


PANEL = jax.ShapeDtypeStruct((256, 128), jnp.float32)


def front_kernel(inv_ref, rhs_ref, coupling_ref, sum_ref, forward_ref):
    j = pl.program_id(0)

    @pl.when(j == 0)
    def _():
        sum_ref[...] = jnp.zeros_like(sum_ref)

    ih, il = two(inv_ref[0])
    rh, rl = two(rhs_ref[0])
    both = jnp.concatenate([rh, rl], axis=1)
    wide = mm(ih, both)
    last = mm(il, both)
    forward = wide[:, :128] + (wide[:, 128:] + (last[:, :128] + last[:, 128:]))
    forward_ref[0] = forward.T
    fh, fl = two(forward)
    both = jnp.concatenate([fh, fl], axis=1)
    for r in range(0, coupling_ref.shape[1], 512):
        ch, cl = two(coupling_ref[0, r : r + 512, :])
        wide = mm(ch, both)
        sum_ref[r : r + 512, :] += wide[:, :128] + wide[:, 128:] + mm(cl, fh)


def front(inv, rhs, coupling):
    return pl.pallas_call(
        front_kernel,
        grid=(8,),
        out_shape=(
            jax.ShapeDtypeStruct((2048, 128), jnp.float32),
            jax.ShapeDtypeStruct((8, 128, 256), jnp.float32),
        ),
        in_specs=[
            pl.BlockSpec((1, 256, 256), lambda j: (j, 0, 0)),
            pl.BlockSpec((1, 256, 128), lambda j: (j, 0, 0)),
            pl.BlockSpec((1, 2048, 256), lambda j: (j, 0, 0)),
        ],
        out_specs=(
            pl.BlockSpec((2048, 128), lambda j: (0, 0)),
            pl.BlockSpec((1, 128, 256), lambda j: (j, 0, 0)),
        ),
        compiler_params=params(60),
        name="leaf_front",
    )(inv, rhs, coupling)


def residual_kernel(top_ref, parts_ref, out_ref):
    value = top_ref[...]
    for p in range(8):
        value = value - parts_ref[p]
    out_ref[...] = value


def residual(top, parts):
    return pl.pallas_call(
        residual_kernel,
        out_shape=PANEL,
        compiler_params=params(16),
        name="residual",
    )(top, parts)


def total_kernel(parts_ref, out_ref):
    value = parts_ref[0]
    for p in range(1, 8):
        value = value + parts_ref[p]
    out_ref[...] = value


def total(parts):
    return pl.pallas_call(
        total_kernel,
        out_shape=jax.ShapeDtypeStruct((128, 256), jnp.float32),
        compiler_params=params(16),
        name="separator",
    )(parts)


def top_kernel(me_ref, inv_ref, *refs):
    res, out_ref = refs[:8], refs[8]
    total = None
    for d in range(8):
        p = (me_ref[0] ^ (d // 2)) * 2 + (me_ref[1] ^ (d % 2))
        th, tl = two(inv_ref[:, pl.ds(pl.multiple_of(p * 256, 256), 256)])
        rh, rl = two(res[d][...])
        wide = mm(th, jnp.concatenate([rh, rl], axis=1))
        term = wide[:, :128] + wide[:, 128:] + mm(tl, rh)
        total = term if total is None else total + term
    fh, fl = two(total.T)
    both = jnp.concatenate([fh, fl], axis=0)
    for p in range(8):
        th, tl = two(inv_ref[:, p * 256 : (p + 1) * 256])
        wide = mm(both, th)
        out_ref[p] = wide[:128] + wide[128:] + mm(fh, tl)


def top(me, inv, res):
    return pl.pallas_call(
        top_kernel,
        grid_spec=pltpu.PrefetchScalarGridSpec(
            num_scalar_prefetch=1,
            grid=(1,),
            in_specs=[pl.BlockSpec((256, 2048), lambda i, me: (0, 0))]
            + [pl.BlockSpec((256, 128), lambda i, me: (0, 0))] * 8,
            out_specs=pl.BlockSpec((8, 128, 256), lambda i, me: (0, 0, 0)),
        ),
        out_shape=jax.ShapeDtypeStruct((8, 128, 256), jnp.float32),
        compiler_params=params(24),
        name="top_solve",
    )(me, inv, *res)


def back_kernel(me_ref, *refs):
    sep, (forward_ref, coupling_ref, inv_ref, cond_ref, out_ref, split_ref, total_ref) = refs[:8], refs[8:]
    j = pl.program_id(0)

    @pl.when(j == 0)
    def _():
        for d in range(8):
            p = (me_ref[0] ^ (d // 2)) * 2 + (me_ref[1] ^ (d % 2))
            split_ref[p, :128], split_ref[p, 128:] = two(sep[d][...])

    total = forward_ref[0]
    for p in range(8):
        ch, cl = two(coupling_ref[0, p * 256 : (p + 1) * 256, :])
        wide = mm(split_ref[p], ch)
        total = total - (wide[:128] + wide[128:] + mm(split_ref[p, :128], cl))
    total_ref[j] = total

    @pl.when(j == 7)
    def _():
        for b in range(8):
            th, tl = two(total_ref[b])
            ih, il = two(inv_ref[b])
            both = jnp.concatenate([th, tl], axis=0)
            wide = mm(both, ih)
            last = mm(both, il)
            field = wide[:128] + (wide[128:] + (last[:128] + last[128:]))
            field = (field * jnp.sqrt(cond_ref[b : b + 1, :])).T
            for c4 in range(4):
                row = (c4 // 2) * 16 + b * 2 + c4 % 2
                out_ref[pl.ds(row, CHIPS, stride=32), :] = field[c4 * CHIPS : (c4 + 1) * CHIPS, :]


def back(me, sep, forward, coupling, inv, cond):
    return pl.pallas_call(
        back_kernel,
        grid_spec=pltpu.PrefetchScalarGridSpec(
            num_scalar_prefetch=1,
            grid=(8,),
            in_specs=[pl.BlockSpec((128, 256), lambda j, me: (0, 0))] * 8
            + [
                pl.BlockSpec((1, 128, 256), lambda j, me: (j, 0, 0)),
                pl.BlockSpec((1, 2048, 256), lambda j, me: (j, 0, 0)),
                pl.BlockSpec((8, 256, 256), lambda j, me: (0, 0, 0)),
                pl.BlockSpec((8, 256), lambda j, me: (0, 0)),
            ],
            out_specs=pl.BlockSpec((CHIPS * 32, 128), lambda j, me: (0, 0)),
            scratch_shapes=[
                pltpu.VMEM((8, 256, 256), jnp.bfloat16),
                pltpu.VMEM((8, 128, 256), jnp.float32),
            ],
        ),
        out_shape=jax.ShapeDtypeStruct((CHIPS * 32, 128), jnp.float32),
        compiler_params=params(48),
        name="leaf_back",
    )(me, *sep, forward, coupling, inv, cond)


def select_kernel(core_ref, el_ref, lists_ref, own_ref, other_ref, out_ref, rows_ref, prod_ref, ids_ref, lanes_ref):
    @pl.when(pl.program_id(0) == 0)
    def _():
        for chip in range(8):
            for ref, core in ((own_ref, core_ref[0]), (other_ref, 1 - core_ref[0])):
                for half in range(2):
                    parts = [ref[chip, p * 32 + half * 16 : p * 32 + half * 16 + 16, :] for p in range(8)]
                    at = (chip * 2 + core) * 256 + half
                    rows_ref[pl.ds(at, 128, stride=2), :] = jnp.concatenate(parts, axis=0).T

    quads_n = prod_ref.shape[0] // 2

    def field(at):
        return rows_ref[pl.ds(pl.multiple_of(el_ref[at], 2), 2), :]

    def load(q):
        a = field(q)
        b = field(quads_n + q)
        c = field(2 * quads_n + q)
        d = field(3 * quads_n + q)
        prod_ref[2 * q : 2 * q + 2, :] = (a - b) * (c - d)

    lane = lax.broadcasted_iota(jnp.int32, (128, 128), 1)
    second = lane & 8 != 0
    upper = lane & 4 != 0
    for pair in range(2):
        for q in range(pair * 256, pair * 256 + 256):
            load(q)
        for t2 in range(2):
            at = (pair * 2 + t2) * 128
            lanes_ref[...] = lists_ref[:16, at : at + 128].astype(jnp.int32) * 2
            for k2 in range(2):
                lanes = lanes_ref[pl.ds(k2, 8, stride=2), :]
                for c2 in range(2):
                    for half in range(2):
                        ids_ref[pl.ds(t2 * 8 + half * 4 + c2 * 2 + k2, 8, stride=16), :] = lanes + c2
        ids = ids_ref[...].T
        tiles = []
        for t2 in range(2):
            for half in range(2):
                prod = prod_ref[pl.ds((pair * 2 + t2) * 256 + half, 128, stride=2), :]
                tiles.append(jnp.take_along_axis(prod, ids, axis=1))
        low = jnp.where(upper, tiles[1], tiles[0])
        high = jnp.where(upper, tiles[3], tiles[2])
        sel = jnp.where(second, high, low).T
        for p in range(8):
            out_ref[p, pair * 16 : (pair + 1) * 16, :] = sel[p * 16 : (p + 1) * 16, :]


def select(core, el, lists, own, other):
    return pl.pallas_call(
        select_kernel,
        grid_spec=pltpu.PrefetchScalarGridSpec(
            num_scalar_prefetch=1,
            grid=(8,),
            in_specs=[
                pl.BlockSpec((2048,), lambda i, core: (i,), memory_space=pltpu.SMEM),
                pl.BlockSpec((32, 512), lambda i, core: (2 * i + core[0], 0)),
                pl.BlockSpec((8, 256, 128), lambda i, core: (0, 0, 0)),
                pl.BlockSpec((8, 256, 128), lambda i, core: (0, 0, 0)),
            ],
            out_specs=pl.BlockSpec((8, 32, 128), lambda i, core: (i, 0, 0)),
            scratch_shapes=[
                pltpu.VMEM((4096, 128), jnp.float32),
                pltpu.VMEM((1024, 128), jnp.float32),
                pltpu.VMEM((128, 128), jnp.int32),
                pltpu.VMEM((16, 128), jnp.int32),
            ],
        ),
        out_shape=jax.ShapeDtypeStruct((CHIPS, 32, 128), jnp.float32),
        compiler_params=params(24),
        name="select_quads",
    )(core, el, lists, own, other)


def assemble_kernel(in_ref, out_ref):
    n = out_ref.shape[2]
    for t in range(4):
        for c4 in range(4):
            for k2 in range(2):
                out_ref[k2, c4, :, t * 128 : (t + 1) * 128] = in_ref[
                    pl.ds(t * 8 + c4 * 2 + k2, n, stride=32), :
                ]


def assemble(received):
    out = pl.pallas_call(
        assemble_kernel,
        grid=(4,),
        out_shape=jax.ShapeDtypeStruct((2, 4, CHIPS, 512), jnp.float32),
        in_specs=[pl.BlockSpec((512, 128), lambda i: (i, 0))],
        out_specs=pl.BlockSpec((2, 4, 16, 512), lambda i: (0, 0, i, 0)),
        compiler_params=params(16),
        name="assemble_sens",
    )(received)
    return out.reshape(2, 256, 512)

def exchange(parts):
    return lax.all_to_all(parts, ("y", "z"), 0, 0, tiled=True)


def send(value, d):
    return lax.ppermute(value, ("y", "z"), [(i, i ^ d) for i in range(8)])


def swap(value, axis):
    return lax.ppermute(value, axis, [(0, 1), (1, 0)])


def all_panels(own):
    far = swap(own, "z")
    return [send(value, 2 * dy) if dy else value for dy in range(4) for value in (own, far)]


def local(leaf_rhs, top_rhs, leaf_inv, coupling, top_inv, cond, electrodes, blocks):
    me = jnp.stack([lax.axis_index("y"), lax.axis_index("z")]).astype(jnp.int32)
    core = lax.axis_index("core").astype(jnp.int32).reshape(1)

    partial_value, forward = front(leaf_inv, leaf_rhs, coupling)
    electrodes, blocks, partial_value = lax.optimization_barrier((electrodes, blocks, partial_value))
    lists = [blocks, electrodes.T * 2, jnp.zeros((12, 512), jnp.int32)]
    lists = jnp.concatenate(lists, axis=0).astype(jnp.float32)
    lists = lax.all_gather(lists, ("chip", "core"), axis=0, tiled=True)
    el = lists.reshape(8, 2, 32, 512)[:, :, 16:20]
    el = jnp.where(core[0] == 1, el[:, 1], el[:, 0]).astype(jnp.int32).reshape(8 * 2048)

    at = (me[0] * 2 + me[1]) * 256
    top_own = lax.dynamic_slice_in_dim(top_rhs, at, 256, 0)
    res = residual(top_own, exchange(partial_value.reshape(8, 256, 128)))
    separator = all_panels(total(exchange(top(me, top_inv, all_panels(res)))))
    separator, el, lists = lax.optimization_barrier((separator, el, lists))

    fields = back(me, separator, forward, coupling, leaf_inv, cond)
    own = lax.all_to_all(fields.reshape(CHIPS, 32, 128), ("chip", "y", "z"), 0, 0, tiled=True)
    own = own.reshape(8, 256, 128)
    other = lax.ppermute(own, "core", [(0, 1), (1, 0)])
    picked = select(core, el, lists, own, other)
    received = lax.all_to_all(picked, ("chip", "y", "z"), 0, 0, tiled=True)
    return assemble(received.reshape(CHIPS * 32, 128))


def solution(mesh):
    devices = np.asarray(mesh.devices)
    fine = Mesh(devices.reshape(8, 2, 4, 2), ("chip", "core", "y", "z"))
    src = ("chip", "core")
    snode = ("y", "z")
    return jax.shard_map(
        local,
        mesh=fine,
        in_specs=(
            P(snode, None, src),
            P(None, src),
            P(snode, None, None),
            P(snode, None, None),
            P(snode, None),
            P(snode, None),
            P(src, None),
            P(None, src),
        ),
        out_specs=P(snode, None, src),
        check_vma=False,
    )
```

```python
import jax
import jax.numpy as jnp
import numpy as np
from jax import lax
from jax.experimental import pallas as pl
from jax.experimental.pallas import tpu as pltpu
from jax.sharding import Mesh, PartitionSpec as P

CHIPS = 64


def two(value):
    high = value.astype(jnp.bfloat16)
    return high, (value - high.astype(jnp.float32)).astype(jnp.bfloat16)


def mm(a, b):
    return jnp.dot(a, b, preferred_element_type=jnp.float32)


def params(mib):
    return pltpu.CompilerParams(vmem_limit_bytes=mib << 20)


PANEL = jax.ShapeDtypeStruct((256, 128), jnp.float32)


def front_kernel(inv_ref, rhs_ref, coupling_ref, sum_ref, forward_ref):
    j = pl.program_id(0)

    @pl.when(j == 0)
    def _():
        sum_ref[...] = jnp.zeros_like(sum_ref)

    ih, il = two(inv_ref[0])
    rh, rl = two(rhs_ref[0])
    both = jnp.concatenate([rh, rl], axis=1)
    wide = mm(ih, both)
    last = mm(il, both)
    forward = wide[:, :128] + (wide[:, 128:] + (last[:, :128] + last[:, 128:]))
    forward_ref[0] = forward.T
    fh, fl = two(forward)
    both = jnp.concatenate([fh, fl], axis=1)
    for r in range(0, coupling_ref.shape[1], 512):
        ch, cl = two(coupling_ref[0, r : r + 512, :])
        wide = mm(ch, both)
        sum_ref[r : r + 512, :] += wide[:, :128] + wide[:, 128:] + mm(cl, fh)


def front(inv, rhs, coupling):
    return pl.pallas_call(
        front_kernel,
        grid=(8,),
        out_shape=(
            jax.ShapeDtypeStruct((2048, 128), jnp.float32),
            jax.ShapeDtypeStruct((8, 128, 256), jnp.float32),
        ),
        in_specs=[
            pl.BlockSpec((1, 256, 256), lambda j: (j, 0, 0)),
            pl.BlockSpec((1, 256, 128), lambda j: (j, 0, 0)),
            pl.BlockSpec((1, 2048, 256), lambda j: (j, 0, 0)),
        ],
        out_specs=(
            pl.BlockSpec((2048, 128), lambda j: (0, 0)),
            pl.BlockSpec((1, 128, 256), lambda j: (j, 0, 0)),
        ),
        compiler_params=params(60),
        name="leaf_front",
    )(inv, rhs, coupling)


def residual_kernel(top_ref, parts_ref, out_ref):
    value = top_ref[...]
    for p in range(8):
        value = value - parts_ref[p]
    out_ref[...] = value


def residual(top, parts):
    return pl.pallas_call(
        residual_kernel,
        out_shape=PANEL,
        compiler_params=params(16),
        name="residual",
    )(top, parts)


def total_kernel(parts_ref, out_ref):
    value = parts_ref[0]
    for p in range(1, 8):
        value = value + parts_ref[p]
    out_ref[...] = value


def total(parts):
    return pl.pallas_call(
        total_kernel,
        out_shape=jax.ShapeDtypeStruct((128, 256), jnp.float32),
        compiler_params=params(16),
        name="separator",
    )(parts)


def top_kernel(me_ref, inv_ref, *refs):
    res, out_ref = refs[:8], refs[8]
    total = None
    for d in range(8):
        p = (me_ref[0] ^ (d // 2)) * 2 + (me_ref[1] ^ (d % 2))
        th, tl = two(inv_ref[:, pl.ds(pl.multiple_of(p * 256, 256), 256)])
        rh, rl = two(res[d][...])
        wide = mm(th, jnp.concatenate([rh, rl], axis=1))
        term = wide[:, :128] + wide[:, 128:] + mm(tl, rh)
        total = term if total is None else total + term
    fh, fl = two(total.T)
    both = jnp.concatenate([fh, fl], axis=0)
    for p in range(8):
        th, tl = two(inv_ref[:, p * 256 : (p + 1) * 256])
        wide = mm(both, th)
        out_ref[p] = wide[:128] + wide[128:] + mm(fh, tl)


def top(me, inv, res):
    return pl.pallas_call(
        top_kernel,
        grid_spec=pltpu.PrefetchScalarGridSpec(
            num_scalar_prefetch=1,
            grid=(1,),
            in_specs=[pl.BlockSpec((256, 2048), lambda i, me: (0, 0))]
            + [pl.BlockSpec((256, 128), lambda i, me: (0, 0))] * 8,
            out_specs=pl.BlockSpec((8, 128, 256), lambda i, me: (0, 0, 0)),
        ),
        out_shape=jax.ShapeDtypeStruct((8, 128, 256), jnp.float32),
        compiler_params=params(24),
        name="top_solve",
    )(me, inv, *res)


def store_split(me_ref, sep, split_ref):
    for d, ref in enumerate(sep):
        cols = pl.ds(pl.multiple_of((d // 2) * 512 + (me_ref[1] ^ (d % 2)) * 256, 256), 256)
        split_ref[:128, cols], split_ref[128:, cols] = two(ref[...])


def minus_terms(total, split_ref, coupling_refs):
    for n, ref in enumerate(coupling_refs):
        cols = slice(n * 512, n * 512 + 512)
        ch, cl = two(ref[0])
        wide = mm(split_ref[:, cols], ch)
        total = total - (wide[:128] + wide[128:] + mm(split_ref[:128, cols], cl))
    return total


def near_kernel(me_ref, own_ref, far_ref, forward_ref, coupling_ref, out_ref, split_ref):
    @pl.when(pl.program_id(0) == 0)
    def _():
        store_split(me_ref, (own_ref, far_ref), split_ref)

    out_ref[0] = minus_terms(forward_ref[0], split_ref, (coupling_ref,))


def panels(dy):
    return pl.BlockSpec((1, 512, 256), lambda j, me: (j, me[0] ^ dy, 0))


def near(me, sep, forward, coupling):
    return pl.pallas_call(
        near_kernel,
        grid_spec=pltpu.PrefetchScalarGridSpec(
            num_scalar_prefetch=1,
            grid=(8,),
            in_specs=[pl.BlockSpec((128, 256), lambda j, me: (0, 0))] * 2
            + [pl.BlockSpec((1, 128, 256), lambda j, me: (j, 0, 0)), panels(0)],
            out_specs=pl.BlockSpec((1, 128, 256), lambda j, me: (j, 0, 0)),
            scratch_shapes=[pltpu.VMEM((256, 512), jnp.bfloat16)],
        ),
        out_shape=jax.ShapeDtypeStruct((8, 128, 256), jnp.float32),
        compiler_params=params(48),
        cost_estimate=pl.CostEstimate(flops=1_000_000_000, bytes_accessed=6_000_000, transcendentals=0),
        name="leaf_near",
    )(me, *sep, forward, coupling)


def back_kernel(me_ref, *refs):
    sep, forward_ref, coupling_refs, (inv_ref, cond_ref, out_ref, split_ref, total_ref) = (
        refs[:6], refs[6], refs[7:10], refs[10:])
    j = pl.program_id(0)

    @pl.when(j == 0)
    def _():
        store_split(me_ref, sep, split_ref)

    total = minus_terms(forward_ref[0], split_ref, coupling_refs)
    total_ref[j] = total

    @pl.when(j == 7)
    def _():
        for b in range(8):
            th, tl = two(total_ref[b])
            ih, il = two(inv_ref[b])
            both = jnp.concatenate([th, tl], axis=0)
            wide = mm(both, ih)
            last = mm(both, il)
            field = wide[:128] + (wide[128:] + (last[:128] + last[128:]))
            field = (field * jnp.sqrt(cond_ref[b : b + 1, :])).T
            for c4 in range(4):
                row = (c4 // 2) * 16 + b * 2 + c4 % 2
                out_ref[pl.ds(row, CHIPS, stride=32), :] = field[c4 * CHIPS : (c4 + 1) * CHIPS, :]


def back(me, sep, forward, coupling, inv, cond):
    return pl.pallas_call(
        back_kernel,
        grid_spec=pltpu.PrefetchScalarGridSpec(
            num_scalar_prefetch=1,
            grid=(8,),
            in_specs=[pl.BlockSpec((128, 256), lambda j, me: (0, 0))] * 6
            + [
                pl.BlockSpec((1, 128, 256), lambda j, me: (j, 0, 0)),
                panels(1),
                panels(2),
                panels(3),
                pl.BlockSpec((8, 256, 256), lambda j, me: (0, 0, 0)),
                pl.BlockSpec((8, 256), lambda j, me: (0, 0)),
            ],
            out_specs=pl.BlockSpec((CHIPS * 32, 128), lambda j, me: (0, 0)),
            scratch_shapes=[
                pltpu.VMEM((256, 1536), jnp.bfloat16),
                pltpu.VMEM((8, 128, 256), jnp.float32),
            ],
        ),
        out_shape=jax.ShapeDtypeStruct((CHIPS * 32, 128), jnp.float32),
        compiler_params=params(48),
        name="leaf_back",
    )(me, *sep, forward, coupling, coupling, coupling, inv, cond)


def select_kernel(core_ref, el_ref, lists_ref, own_ref, other_ref, out_ref, rows_ref, prod_ref, ids_ref, lanes_ref):
    @pl.when(pl.program_id(0) == 0)
    def _():
        for chip in range(8):
            for ref, core in ((own_ref, core_ref[0]), (other_ref, 1 - core_ref[0])):
                for half in range(2):
                    parts = [ref[chip, p * 32 + half * 16 : p * 32 + half * 16 + 16, :] for p in range(8)]
                    at = (chip * 2 + core) * 256 + half
                    rows_ref[pl.ds(at, 128, stride=2), :] = jnp.concatenate(parts, axis=0).T

    quads_n = prod_ref.shape[0] // 2

    def field(at):
        return rows_ref[pl.ds(pl.multiple_of(el_ref[at], 2), 2), :]

    def load(q):
        a = field(q)
        b = field(quads_n + q)
        c = field(2 * quads_n + q)
        d = field(3 * quads_n + q)
        prod_ref[2 * q : 2 * q + 2, :] = (a - b) * (c - d)

    lane = lax.broadcasted_iota(jnp.int32, (128, 128), 1)
    second = lane & 8 != 0
    upper = lane & 4 != 0
    for pair in range(2):
        for q in range(pair * 256, pair * 256 + 256):
            load(q)
        for t2 in range(2):
            at = (pair * 2 + t2) * 128
            lanes_ref[...] = lists_ref[:16, at : at + 128].astype(jnp.int32) * 2
            for k2 in range(2):
                lanes = lanes_ref[pl.ds(k2, 8, stride=2), :]
                for c2 in range(2):
                    for half in range(2):
                        ids_ref[pl.ds(t2 * 8 + half * 4 + c2 * 2 + k2, 8, stride=16), :] = lanes + c2
        ids = ids_ref[...].T
        tiles = []
        for t2 in range(2):
            for half in range(2):
                prod = prod_ref[pl.ds((pair * 2 + t2) * 256 + half, 128, stride=2), :]
                tiles.append(jnp.take_along_axis(prod, ids, axis=1))
        low = jnp.where(upper, tiles[1], tiles[0])
        high = jnp.where(upper, tiles[3], tiles[2])
        sel = jnp.where(second, high, low).T
        for p in range(8):
            out_ref[p, pair * 16 : (pair + 1) * 16, :] = sel[p * 16 : (p + 1) * 16, :]


def select(core, el, lists, own, other):
    return pl.pallas_call(
        select_kernel,
        grid_spec=pltpu.PrefetchScalarGridSpec(
            num_scalar_prefetch=1,
            grid=(8,),
            in_specs=[
                pl.BlockSpec((2048,), lambda i, core: (i,), memory_space=pltpu.SMEM),
                pl.BlockSpec((32, 512), lambda i, core: (2 * i + core[0], 0)),
                pl.BlockSpec((8, 256, 128), lambda i, core: (0, 0, 0)),
                pl.BlockSpec((8, 256, 128), lambda i, core: (0, 0, 0)),
            ],
            out_specs=pl.BlockSpec((8, 32, 128), lambda i, core: (i, 0, 0)),
            scratch_shapes=[
                pltpu.VMEM((4096, 128), jnp.float32),
                pltpu.VMEM((1024, 128), jnp.float32),
                pltpu.VMEM((128, 128), jnp.int32),
                pltpu.VMEM((16, 128), jnp.int32),
            ],
        ),
        out_shape=jax.ShapeDtypeStruct((CHIPS, 32, 128), jnp.float32),
        compiler_params=params(24),
        name="select_quads",
    )(core, el, lists, own, other)


def assemble_kernel(in_ref, out_ref):
    n = out_ref.shape[2]
    for t in range(4):
        for c4 in range(4):
            for k2 in range(2):
                out_ref[k2, c4, :, t * 128 : (t + 1) * 128] = in_ref[
                    pl.ds(t * 8 + c4 * 2 + k2, n, stride=32), :
                ]


def assemble(received):
    out = pl.pallas_call(
        assemble_kernel,
        grid=(4,),
        out_shape=jax.ShapeDtypeStruct((2, 4, CHIPS, 512), jnp.float32),
        in_specs=[pl.BlockSpec((512, 128), lambda i: (i, 0))],
        out_specs=pl.BlockSpec((2, 4, 16, 512), lambda i: (0, 0, i, 0)),
        compiler_params=params(16),
        name="assemble_sens",
    )(received)
    return out.reshape(2, 256, 512)

def exchange(parts):
    return lax.all_to_all(parts, ("y", "z"), 0, 0, tiled=True)


def send(value, d):
    return lax.ppermute(value, ("y", "z"), [(i, i ^ d) for i in range(8)])


def swap(value, axis):
    return lax.ppermute(value, axis, [(0, 1), (1, 0)])


def all_panels(own):
    far = swap(own, "z")
    return [send(value, 2 * dy) if dy else value for dy in range(4) for value in (own, far)]


def local(leaf_rhs, top_rhs, leaf_inv, coupling, top_inv, cond, electrodes, blocks):
    me = jnp.stack([lax.axis_index("y"), lax.axis_index("z")]).astype(jnp.int32)
    core = lax.axis_index("core").astype(jnp.int32).reshape(1)

    partial_value, forward = front(leaf_inv, leaf_rhs, coupling)
    electrodes, blocks, partial_value = lax.optimization_barrier((electrodes, blocks, partial_value))
    lists = [blocks, electrodes.T * 2, jnp.zeros((12, 512), jnp.int32)]
    lists = jnp.concatenate(lists, axis=0).astype(jnp.float32)
    lists = lax.all_gather(lists, ("chip", "core"), axis=0, tiled=True)
    el = lists.reshape(8, 2, 32, 512)[:, :, 16:20]
    el = jnp.where(core[0] == 1, el[:, 1], el[:, 0]).astype(jnp.int32).reshape(8 * 2048)

    at = (me[0] * 2 + me[1]) * 256
    top_own = lax.dynamic_slice_in_dim(top_rhs, at, 256, 0)
    res = residual(top_own, exchange(partial_value.reshape(8, 256, 128)))
    separator = all_panels(total(exchange(top(me, top_inv, all_panels(res)))))
    started = near(me, separator[:2], forward, coupling)
    separator, el, lists = lax.optimization_barrier((separator, el, lists))

    fields = back(me, separator[2:], started, coupling, leaf_inv, cond)
    own = lax.all_to_all(fields.reshape(CHIPS, 32, 128), ("chip", "y", "z"), 0, 0, tiled=True)
    own = own.reshape(8, 256, 128)
    other = lax.ppermute(own, "core", [(0, 1), (1, 0)])
    picked = select(core, el, lists, own, other)
    received = lax.all_to_all(picked, ("chip", "y", "z"), 0, 0, tiled=True)
    return assemble(received.reshape(CHIPS * 32, 128))


def solution(mesh):
    devices = np.asarray(mesh.devices)
    fine = Mesh(devices.reshape(8, 2, 4, 2), ("chip", "core", "y", "z"))
    src = ("chip", "core")
    snode = ("y", "z")
    return jax.shard_map(
        local,
        mesh=fine,
        in_specs=(
            P(snode, None, src),
            P(None, src),
            P(snode, None, None),
            P(snode, None, None),
            P(snode, None),
            P(snode, None),
            P(src, None),
            P(None, src),
        ),
        out_specs=P(snode, None, src),
        check_vma=False,
    )
```

```python
import jax
import jax.numpy as jnp
import numpy as np
from jax import lax
from jax.experimental import pallas as pl
from jax.experimental.pallas import tpu as pltpu
from jax.sharding import Mesh, PartitionSpec as P

CHIPS = 64


def two(value):
    high = value.astype(jnp.bfloat16)
    return high, (value - high.astype(jnp.float32)).astype(jnp.bfloat16)


def mm(a, b):
    return jnp.dot(a, b, preferred_element_type=jnp.float32)


def params(mib):
    return pltpu.CompilerParams(vmem_limit_bytes=mib << 20)


PANEL = jax.ShapeDtypeStruct((256, 128), jnp.float32)


def front_kernel(inv_ref, rhs_ref, coupling_ref, sum_ref, forward_ref):
    j = pl.program_id(0)

    @pl.when(j == 0)
    def _():
        sum_ref[...] = jnp.zeros_like(sum_ref)

    ih, il = two(inv_ref[0])
    rh, rl = two(rhs_ref[0])
    both = jnp.concatenate([rh, rl], axis=1)
    wide = mm(ih, both)
    last = mm(il, both)
    forward = wide[:, :128] + (wide[:, 128:] + (last[:, :128] + last[:, 128:]))
    forward_ref[0] = forward.T
    fh, fl = two(forward)
    both = jnp.concatenate([fh, fl], axis=1)
    for r in range(0, coupling_ref.shape[1], 512):
        ch, cl = two(coupling_ref[0, r : r + 512, :])
        wide = mm(ch, both)
        sum_ref[r : r + 512, :] += wide[:, :128] + wide[:, 128:] + mm(cl, fh)


def front(inv, rhs, coupling):
    return pl.pallas_call(
        front_kernel,
        grid=(8,),
        out_shape=(
            jax.ShapeDtypeStruct((2048, 128), jnp.float32),
            jax.ShapeDtypeStruct((8, 128, 256), jnp.float32),
        ),
        in_specs=[
            pl.BlockSpec((1, 256, 256), lambda j: (j, 0, 0)),
            pl.BlockSpec((1, 256, 128), lambda j: (j, 0, 0)),
            pl.BlockSpec((1, 2048, 256), lambda j: (j, 0, 0)),
        ],
        out_specs=(
            pl.BlockSpec((2048, 128), lambda j: (0, 0)),
            pl.BlockSpec((1, 128, 256), lambda j: (j, 0, 0)),
        ),
        compiler_params=params(60),
        name="leaf_front",
    )(inv, rhs, coupling)


def residual_kernel(top_ref, parts_ref, out_ref):
    value = top_ref[...]
    for p in range(8):
        value = value - parts_ref[p]
    out_ref[...] = value


def residual(top, parts):
    return pl.pallas_call(
        residual_kernel,
        out_shape=PANEL,
        compiler_params=params(16),
        name="residual",
    )(top, parts)


def total_kernel(parts_ref, out_ref):
    value = parts_ref[0]
    for p in range(1, 8):
        value = value + parts_ref[p]
    out_ref[...] = value


def total(parts):
    return pl.pallas_call(
        total_kernel,
        out_shape=jax.ShapeDtypeStruct((128, 256), jnp.float32),
        compiler_params=params(16),
        name="separator",
    )(parts)


def top_kernel(me_ref, inv_ref, *refs):
    res, out_ref = refs[:8], refs[8]
    total = None
    for d in range(8):
        p = (me_ref[0] ^ (d // 2)) * 2 + (me_ref[1] ^ (d % 2))
        th, tl = two(inv_ref[:, pl.ds(pl.multiple_of(p * 256, 256), 256)])
        rh, rl = two(res[d][...])
        wide = mm(th, jnp.concatenate([rh, rl], axis=1))
        term = wide[:, :128] + wide[:, 128:] + mm(tl, rh)
        total = term if total is None else total + term
    fh, fl = two(total.T)
    both = jnp.concatenate([fh, fl], axis=0)
    for p in range(8):
        th, tl = two(inv_ref[:, p * 256 : (p + 1) * 256])
        wide = mm(both, th)
        out_ref[p] = wide[:128] + wide[128:] + mm(fh, tl)


def top(me, inv, res):
    return pl.pallas_call(
        top_kernel,
        grid_spec=pltpu.PrefetchScalarGridSpec(
            num_scalar_prefetch=1,
            grid=(1,),
            in_specs=[pl.BlockSpec((256, 2048), lambda i, me: (0, 0))]
            + [pl.BlockSpec((256, 128), lambda i, me: (0, 0))] * 8,
            out_specs=pl.BlockSpec((8, 128, 256), lambda i, me: (0, 0, 0)),
        ),
        out_shape=jax.ShapeDtypeStruct((8, 128, 256), jnp.float32),
        compiler_params=params(24),
        name="top_solve",
    )(me, inv, *res)


def store_split(me_ref, sep, split_ref):
    for d, ref in enumerate(sep):
        cols = pl.ds(pl.multiple_of((d // 2) * 512 + (me_ref[1] ^ (d % 2)) * 256, 256), 256)
        split_ref[:128, cols], split_ref[128:, cols] = two(ref[...])


def minus_terms(total, split_ref, coupling_refs):
    for n, ref in enumerate(coupling_refs):
        cols = slice(n * 512, n * 512 + 512)
        ch, cl = two(ref[0])
        wide = mm(split_ref[:, cols], ch)
        total = total - (wide[:128] + wide[128:] + mm(split_ref[:128, cols], cl))
    return total


def near_kernel(me_ref, own_ref, far_ref, forward_ref, coupling_ref, out_ref, split_ref):
    @pl.when(pl.program_id(0) == 0)
    def _():
        store_split(me_ref, (own_ref, far_ref), split_ref)

    for b in range(2):
        out_ref[b] = minus_terms(forward_ref[b], split_ref, (coupling_ref.at[b : b + 1],))


def panels(dy):
    return pl.BlockSpec((1, 512, 256), lambda j, me: (j, me[0] ^ dy, 0))


def near(me, sep, forward, coupling):
    return pl.pallas_call(
        near_kernel,
        grid_spec=pltpu.PrefetchScalarGridSpec(
            num_scalar_prefetch=1,
            grid=(4,),
            in_specs=[pl.BlockSpec((128, 256), lambda j, me: (0, 0))] * 2
            + [pl.BlockSpec((2, 128, 256), lambda j, me: (j, 0, 0))]
            + [pl.BlockSpec((2, 512, 256), lambda j, me: (j, me[0], 0))],
            out_specs=pl.BlockSpec((2, 128, 256), lambda j, me: (j, 0, 0)),
            scratch_shapes=[pltpu.VMEM((256, 512), jnp.bfloat16)],
        ),
        out_shape=jax.ShapeDtypeStruct((8, 128, 256), jnp.float32),
        compiler_params=params(48),
        cost_estimate=pl.CostEstimate(flops=1_000_000_000, bytes_accessed=6_000_000, transcendentals=0),
        name="leaf_near",
    )(me, *sep, forward, coupling)


def back_kernel(me_ref, *refs):
    sep, forward_ref, coupling_refs, (inv_ref, cond_ref, out_ref, split_ref, total_ref) = (
        refs[:6], refs[6], refs[7:10], refs[10:])
    j = pl.program_id(0)

    @pl.when(j == 0)
    def _():
        store_split(me_ref, sep, split_ref)

    total = minus_terms(forward_ref[0], split_ref, coupling_refs)
    total_ref[j] = total

    @pl.when(j == 7)
    def _():
        for b in range(8):
            th, tl = two(total_ref[b])
            ih, il = two(inv_ref[b])
            both = jnp.concatenate([th, tl], axis=0)
            wide = mm(both, ih)
            last = mm(both, il)
            field = wide[:128] + (wide[128:] + (last[:128] + last[128:]))
            field = (field * jnp.sqrt(cond_ref[b : b + 1, :])).T
            for c4 in range(4):
                row = (c4 // 2) * 16 + b * 2 + c4 % 2
                out_ref[pl.ds(row, CHIPS, stride=32), :] = field[c4 * CHIPS : (c4 + 1) * CHIPS, :]


def back(me, sep, forward, coupling, inv, cond):
    return pl.pallas_call(
        back_kernel,
        grid_spec=pltpu.PrefetchScalarGridSpec(
            num_scalar_prefetch=1,
            grid=(8,),
            in_specs=[pl.BlockSpec((128, 256), lambda j, me: (0, 0))] * 6
            + [
                pl.BlockSpec((1, 128, 256), lambda j, me: (j, 0, 0)),
                panels(1),
                panels(2),
                panels(3),
                pl.BlockSpec((8, 256, 256), lambda j, me: (0, 0, 0)),
                pl.BlockSpec((8, 256), lambda j, me: (0, 0)),
            ],
            out_specs=pl.BlockSpec((CHIPS * 32, 128), lambda j, me: (0, 0)),
            scratch_shapes=[
                pltpu.VMEM((256, 1536), jnp.bfloat16),
                pltpu.VMEM((8, 128, 256), jnp.float32),
            ],
        ),
        out_shape=jax.ShapeDtypeStruct((CHIPS * 32, 128), jnp.float32),
        compiler_params=params(48),
        name="leaf_back",
    )(me, *sep, forward, coupling, coupling, coupling, inv, cond)


def select_kernel(core_ref, el_ref, lists_ref, own_ref, other_ref, out_ref, rows_ref, prod_ref, ids_ref, lanes_ref):
    @pl.when(pl.program_id(0) == 0)
    def _():
        for chip in range(8):
            for ref, core in ((own_ref, core_ref[0]), (other_ref, 1 - core_ref[0])):
                for half in range(2):
                    parts = [ref[chip, p * 32 + half * 16 : p * 32 + half * 16 + 16, :] for p in range(8)]
                    at = (chip * 2 + core) * 256 + half
                    rows_ref[pl.ds(at, 128, stride=2), :] = jnp.concatenate(parts, axis=0).T

    quads_n = prod_ref.shape[0] // 2

    def field(at):
        return rows_ref[pl.ds(pl.multiple_of(el_ref[at], 2), 2), :]

    def load(q):
        a = field(q)
        b = field(quads_n + q)
        c = field(2 * quads_n + q)
        d = field(3 * quads_n + q)
        prod_ref[2 * q : 2 * q + 2, :] = (a - b) * (c - d)

    lane = lax.broadcasted_iota(jnp.int32, (128, 128), 1)
    second = lane & 8 != 0
    upper = lane & 4 != 0
    for pair in range(2):
        for q in range(pair * 256, pair * 256 + 256):
            load(q)
        for t2 in range(2):
            at = (pair * 2 + t2) * 128
            lanes_ref[...] = lists_ref[:16, at : at + 128].astype(jnp.int32) * 2
            for k2 in range(2):
                lanes = lanes_ref[pl.ds(k2, 8, stride=2), :]
                for c2 in range(2):
                    for half in range(2):
                        ids_ref[pl.ds(t2 * 8 + half * 4 + c2 * 2 + k2, 8, stride=16), :] = lanes + c2
        ids = ids_ref[...].T
        tiles = []
        for t2 in range(2):
            for half in range(2):
                prod = prod_ref[pl.ds((pair * 2 + t2) * 256 + half, 128, stride=2), :]
                tiles.append(jnp.take_along_axis(prod, ids, axis=1))
        low = jnp.where(upper, tiles[1], tiles[0])
        high = jnp.where(upper, tiles[3], tiles[2])
        sel = jnp.where(second, high, low).T
        for p in range(8):
            out_ref[p, pair * 16 : (pair + 1) * 16, :] = sel[p * 16 : (p + 1) * 16, :]


def select(core, el, lists, own, other):
    return pl.pallas_call(
        select_kernel,
        grid_spec=pltpu.PrefetchScalarGridSpec(
            num_scalar_prefetch=1,
            grid=(8,),
            in_specs=[
                pl.BlockSpec((2048,), lambda i, core: (i,), memory_space=pltpu.SMEM),
                pl.BlockSpec((32, 512), lambda i, core: (2 * i + core[0], 0)),
                pl.BlockSpec((8, 256, 128), lambda i, core: (0, 0, 0)),
                pl.BlockSpec((8, 256, 128), lambda i, core: (0, 0, 0)),
            ],
            out_specs=pl.BlockSpec((8, 32, 128), lambda i, core: (i, 0, 0)),
            scratch_shapes=[
                pltpu.VMEM((4096, 128), jnp.float32),
                pltpu.VMEM((1024, 128), jnp.float32),
                pltpu.VMEM((128, 128), jnp.int32),
                pltpu.VMEM((16, 128), jnp.int32),
            ],
        ),
        out_shape=jax.ShapeDtypeStruct((CHIPS, 32, 128), jnp.float32),
        compiler_params=params(24),
        name="select_quads",
    )(core, el, lists, own, other)


def assemble_kernel(in_ref, out_ref):
    n = out_ref.shape[2]
    for t in range(4):
        for c4 in range(4):
            for k2 in range(2):
                out_ref[k2, c4, :, t * 128 : (t + 1) * 128] = in_ref[
                    pl.ds(t * 8 + c4 * 2 + k2, n, stride=32), :
                ]


def assemble(received):
    out = pl.pallas_call(
        assemble_kernel,
        grid=(4,),
        out_shape=jax.ShapeDtypeStruct((2, 4, CHIPS, 512), jnp.float32),
        in_specs=[pl.BlockSpec((512, 128), lambda i: (i, 0))],
        out_specs=pl.BlockSpec((2, 4, 16, 512), lambda i: (0, 0, i, 0)),
        compiler_params=params(16),
        name="assemble_sens",
    )(received)
    return out.reshape(2, 256, 512)

def exchange(parts):
    return lax.all_to_all(parts, ("y", "z"), 0, 0, tiled=True)


def send(value, d):
    return lax.ppermute(value, ("y", "z"), [(i, i ^ d) for i in range(8)])


def swap(value, axis):
    return lax.ppermute(value, axis, [(0, 1), (1, 0)])


def all_panels(own):
    far = swap(own, "z")
    return [send(value, 2 * dy) if dy else value for dy in range(4) for value in (own, far)]


def local(leaf_rhs, top_rhs, leaf_inv, coupling, top_inv, cond, electrodes, blocks):
    me = jnp.stack([lax.axis_index("y"), lax.axis_index("z")]).astype(jnp.int32)
    core = lax.axis_index("core").astype(jnp.int32).reshape(1)

    partial_value, forward = front(leaf_inv, leaf_rhs, coupling)
    electrodes, blocks, partial_value = lax.optimization_barrier((electrodes, blocks, partial_value))
    lists = [blocks, electrodes.T * 2, jnp.zeros((12, 512), jnp.int32)]
    lists = jnp.concatenate(lists, axis=0).astype(jnp.float32)
    lists = lax.all_gather(lists, ("chip", "core"), axis=0, tiled=True)
    el = lists.reshape(8, 2, 32, 512)[:, :, 16:20]
    el = jnp.where(core[0] == 1, el[:, 1], el[:, 0]).astype(jnp.int32).reshape(8 * 2048)

    at = (me[0] * 2 + me[1]) * 256
    top_own = lax.dynamic_slice_in_dim(top_rhs, at, 256, 0)
    res = residual(top_own, exchange(partial_value.reshape(8, 256, 128)))
    separator = all_panels(total(exchange(top(me, top_inv, all_panels(res)))))
    started = near(me, separator[:2], forward, coupling)
    separator, el, lists = lax.optimization_barrier((separator, el, lists))

    fields = back(me, separator[2:], started, coupling, leaf_inv, cond)
    own = lax.all_to_all(fields.reshape(CHIPS, 32, 128), ("chip", "y", "z"), 0, 0, tiled=True)
    own = own.reshape(8, 256, 128)
    other = lax.ppermute(own, "core", [(0, 1), (1, 0)])
    picked = select(core, el, lists, own, other)
    received = lax.all_to_all(picked, ("chip", "y", "z"), 0, 0, tiled=True)
    return assemble(received.reshape(CHIPS * 32, 128))


def solution(mesh):
    devices = np.asarray(mesh.devices)
    fine = Mesh(devices.reshape(8, 2, 4, 2), ("chip", "core", "y", "z"))
    src = ("chip", "core")
    snode = ("y", "z")
    return jax.shard_map(
        local,
        mesh=fine,
        in_specs=(
            P(snode, None, src),
            P(None, src),
            P(snode, None, None),
            P(snode, None, None),
            P(snode, None),
            P(snode, None),
            P(src, None),
            P(None, src),
        ),
        out_specs=P(snode, None, src),
        check_vma=False,
    )
```
